32 devices in a mesh: ctx: 8 (over z, x), head: 4 (over y, core).
Axes of the slice: x: 2, y: 2, z: 4, core: 2. Of those that a mesh axis runs over, the one named last changes fastest.
Arguments:
- queries: bfloat16 [3072, 8192], P('ctx', 'head'), may hold values from -160 to 160
- keys: bfloat16 [3072, 1024], P('ctx', 'head'), may hold values from -4 to 4
- values: bfloat16 [3072, 1024], P('ctx', 'head'), may hold values from -6 to 6
- keep_rows: int32 [8, 8, 8, 4], P('ctx', 'head'), may hold values from 0 to 383
- keep_dest: int32 [8, 8, 8], P('ctx', 'head'), may hold values from 0 to 7, as said below
- keep_count: int32 [8, 8, 8], P('ctx', 'head'), may hold values from 1 to 4, as said below
Outputs:
- attended: bfloat16 [3072, 8192], P('ctx', 'head')
- key_scores: float32 [3072], P('ctx')
- decode_cache: bfloat16 [8, 8, 4, 8, 256], P('ctx', None, None, 'head')
The draws below stay inside these ranges and needn't reach their ends.
Inputs may be any that keep to these rules, and one draw needn't show every extreme that they name: For each source shard and head, keep_dest over j is a permutation of 0 to 7. `keep_count`: in every draw some decode shard receives 4 live slots in every block.
All inputs are finite; a program needn't handle non-finite values.
Results may differ from the reference program's by a relative error of at most 0.0045.
Values may be sent and summed in bfloat16 or wider, within the bound.
No kernel may reach another device: no remote copies, remote signals or barrier semaphores. Data moves between devices by JAX's collectives and lax.ppermute only.
A program may use at most 64 MiB of HBM per device.

```python
import jax
import jax.numpy as jnp
from jax import lax

HD = 128
KVH = 8
QPK = 8
BLK = 192
KB = 4
QH = 64
TOK_DEV = 384
TOKENS = 3072
N_CTX = 8


def shared_keys(key):
    key = jax.random.fold_in(key, 101)
    return jnp.clip(jax.random.normal(key, (TOKENS, KVH * HD), jnp.float32), -4.0, 4.0)


def destinations(key):
    key = jax.random.fold_in(key, 202)
    bits = jax.random.randint(key, (N_CTX, KVH, N_CTX), 0, 1 << 20)
    ranked = bits * N_CTX + jnp.arange(N_CTX, dtype=jnp.int32)
    return jnp.argsort(ranked, axis=-1).astype(jnp.int32)


def draw_keys(key, part):
    return shared_keys(key).astype(jnp.bfloat16)


def draw_queries(key, part):
    key = jax.random.fold_in(key, 11)
    found = jnp.clip(jax.random.normal(key, (TOKENS, QH * HD), jnp.float32), -6.0, 6.0)
    return found.astype(jnp.bfloat16)


def draw_keep_dest(key, part):
    return destinations(key)


def draw_keep_count(key, part):
    dest = destinations(key)
    key = jax.random.fold_in(key, 5)
    first, second = jax.random.split(key)
    counts = jax.random.randint(first, (N_CTX, KVH, N_CTX), 1, KB + 1)
    chosen = jax.random.randint(second, (), 0, N_CTX)
    return jnp.where(dest == chosen, KB, counts).astype(jnp.int32)


def place_ends(entries, stream_key, low, top_value):
    place = [jax.random.randint(jax.random.fold_in(stream_key, axis), (), 0, length) for axis, length in enumerate(entries.shape)]
    longest = entries.shape.index(max(entries.shape))
    next_to = place[:longest] + [(place[longest] + 1) % entries.shape[longest]] + place[longest + 1:]
    return entries.at[tuple(place)].set(low).at[tuple(next_to)].set(top_value)


def shard_levels(stream_key, shape, cuts, low, top_value):
    def one(axis_at, shards_of):
        steps = jax.random.uniform(jax.random.fold_in(jax.random.fold_in(stream_key, 6), axis_at), (shards_of,), jnp.float32, low / len(cuts), top_value / len(cuts))
        return jnp.repeat(jnp.exp(steps), shape[axis_at] // shards_of).reshape((-1,) + (1,) * (len(shape) - axis_at - 1))

    gain = one(*cuts[0])
    for cut in cuts[1:]:
        gain = gain * one(*cut)
    return gain


def bell_draw(own_key, shape, width, most, cuts=(), held_as=jnp.bfloat16):
    drawn = width * jax.random.normal(own_key, shape, jnp.float32)
    if cuts:
        drawn = drawn * shard_levels(own_key, shape, cuts, -0.22, 0.18)
    return jnp.clip(drawn, -most, most).astype(held_as)


def setup_inputs(seed: int = 0) -> dict:
    key_of = jax.random.split(jax.random.key(seed), 7)
    queries = draw_queries(jax.random.fold_in(key_of[6], 71), 0)
    keys = draw_keys(jax.random.fold_in(key_of[6], 71), 0)
    values = bell_draw(key_of[2], (TOKENS, KVH * HD), 1.0, 6.0, ((0, 8), (1, 4)))
    keep_rows = place_ends(jax.random.randint(key_of[3], (N_CTX, KVH, N_CTX, KB), 0, TOK_DEV), jax.random.fold_in(key_of[3], 1), 0, TOK_DEV - 1).astype(jnp.int32)
    keep_dest = draw_keep_dest(jax.random.fold_in(key_of[6], 71), 0)
    keep_count = draw_keep_count(jax.random.fold_in(key_of[6], 71), 0)
    return dict(queries=queries, keys=keys, values=values, keep_rows=keep_rows, keep_dest=keep_dest, keep_count=keep_count)


def block_positions(shard, half):
    index = jnp.arange(2 * half, dtype=jnp.int32)
    return jnp.where(index < half, shard * half + index, (2 * N_CTX - 1 - shard) * half + index - half).astype(jnp.int32)


def reference(queries, keys, values, keep_rows, keep_dest, keep_count):
    tok = 2 * BLK
    scale = HD ** -0.5
    q_shards = queries.reshape(N_CTX, tok, KVH, QPK, HD)
    k_shards = keys.reshape(N_CTX, tok, KVH, HD)
    v_shards = values.reshape(N_CTX, tok, KVH, HD)

    def one_shard(shard):
        sources = [((shard - step) % N_CTX).astype(jnp.int32) for step in range(3)]
        key_cat = jnp.concatenate([lax.dynamic_index_in_dim(k_shards, s, 0, keepdims=False) for s in sources], 0).astype(jnp.float32)
        val_cat = jnp.concatenate([lax.dynamic_index_in_dim(v_shards, s, 0, keepdims=False) for s in sources], 0).astype(jnp.float32)
        key_pos = jnp.concatenate([block_positions(s, BLK) for s in sources])
        query_pos = block_positions(shard, BLK)
        query_blk = lax.dynamic_index_in_dim(q_shards, shard, 0, keepdims=False).astype(jnp.float32)
        score = jnp.einsum('qgrd,kgd->grqk', query_blk, key_cat) * scale
        score = jnp.where((key_pos[None, :] <= query_pos[:, None])[None, None], score, -jnp.inf)
        top = jnp.max(score, -1, keepdims=True)
        weight = jnp.exp(score - top)
        total = jnp.sum(weight, -1, keepdims=True)
        rounded = lax.optimization_barrier(weight.astype(jnp.bfloat16)).astype(jnp.float32)
        product = jnp.einsum('grqk,kgd->grqd', rounded, val_cat) / total
        output = jnp.transpose(product, (2, 0, 1, 3)).reshape(tok, KVH * QPK * HD).astype(jnp.bfloat16)
        column = jnp.sum(weight / total, axis=(0, 1, 2)) / QH
        return output, column.reshape(3, tok)

    outputs, columns = lax.map(one_shard, jnp.arange(N_CTX, dtype=jnp.int32))
    attended = outputs.reshape(N_CTX * tok, KVH * QPK * HD)
    key_scores = columns[:, 0] + jnp.roll(columns[:, 1], -1, 0) + jnp.roll(columns[:, 2], -2, 0)
    key_scores = key_scores.reshape(N_CTX * tok)

    pairs = jnp.concatenate([k_shards, v_shards], axis=3)
    head_index = jnp.arange(KVH, dtype=jnp.int32)
    block_index = jnp.arange(N_CTX, dtype=jnp.int32)

    def one_source(shard):
        local = lax.dynamic_index_in_dim(pairs, shard, 0, keepdims=False)
        rows = lax.dynamic_index_in_dim(keep_rows, shard, 0, keepdims=False)
        dest = lax.dynamic_index_in_dim(keep_dest, shard, 0, keepdims=False)
        live = lax.dynamic_index_in_dim(keep_count, shard, 0, keepdims=False)
        picked = local[rows, head_index[:, None, None]]
        slot = jnp.arange(KB, dtype=jnp.int32)
        picked = jnp.where((slot[None, None, :] < live[:, :, None])[..., None], picked, jnp.zeros((), jnp.bfloat16))
        match = dest[:, :, None] == block_index[None, None, :]
        inverse = jnp.sum(block_index[None, :, None] * match, axis=1).astype(jnp.int32)
        return picked[head_index[:, None], inverse]

    sent = lax.map(one_source, jnp.arange(N_CTX, dtype=jnp.int32))
    decode_cache = jnp.transpose(sent, (2, 0, 3, 1, 4))
    return attended, key_scores, decode_cache
```

```python
import functools
import math

import jax
import jax.numpy as jnp
from jax import lax
from jax.experimental import pallas as pl
from jax.experimental.pallas import tpu as pltpu
from jax.sharding import PartitionSpec as P

HD = 128
KB = 4
QH = 64
LANES = 128
CHUNK = 32
STEP_HEADS = 4
EXP2_SCALE = HD ** (-0.5) * math.log2(math.e)
VMEM = pl.BlockSpec(memory_space=pltpu.VMEM)
HBM = pl.BlockSpec(memory_space=pltpu.HBM)
MIB = 1024 * 1024


def tiles(width):
    return pl.cdiv(width, LANES) * LANES


def wide(column):
    return jnp.broadcast_to(column, (CHUNK, LANES))


def folded(block):
    return jnp.sum(block.reshape(-1, 8, LANES), axis=0)


def pick_rows(groups, k_ref, v_ref, rows_ref, dest_ref, live_ref, kept_ref, sent_ref, onehot):
    tok = k_ref.shape[0]
    me = lax.axis_index("ctx")
    count = dest_ref.shape[2]
    bits = count.bit_length() - 2
    size = kept_ref.shape[0]
    lanes = lax.broadcasted_iota(jnp.int32, (1, tok), 1)
    onehot[...] = jnp.zeros_like(onehot)
    for group in range(groups):
        @pl.loop(0, count, unroll=4)
        def _(j):
            dest = dest_ref[0, group, j]
            place = (dest + me) % 2
            for bit in range(bits):
                place = 2 * place + (dest >> (bit + 1)) % 2
            for slot in range(KB):
                row = jnp.where(slot < live_ref[0, group, j], rows_ref[0, group, slot, j], -1)
                at = (place * KB + slot) * groups + group
                onehot[group, pl.ds(at, 1)] = (lanes == row).astype(jnp.float32)
    for first, picked_ref in ((0, kept_ref), (size, sent_ref)):
        for ref, lane in ((k_ref, 0), (v_ref, HD)):
            picked_ref[:, lane : lane + HD] = sum(
                jnp.dot(
                    onehot[group, first : first + size].astype(jnp.bfloat16),
                    ref[:, group * HD : (group + 1) * HD],
                    preferred_element_type=jnp.float32,
                )
                for group in range(groups)
            ).astype(jnp.bfloat16)


def keep_kernel(groups, k_ref, v_ref, rows_hbm, dest_hbm, live_hbm, kept_ref, again1_ref, again2_ref, *refs):
    tok = k_ref.shape[0]
    *bit_refs, rows_ref, dest_ref, live_ref, onehot, sems = refs
    me = lax.axis_index("ctx")
    for bit, bit_ref in enumerate(bit_refs):
        bit_ref[...] = jnp.broadcast_to((me >> bit) % 2, bit_ref.shape)
    copies = [
        pltpu.make_async_copy(src, dst, sems.at[i])
        for i, (src, dst) in enumerate(
            ((rows_hbm, rows_ref), (dest_hbm, dest_ref), (live_hbm, live_ref))
        )
    ]
    for copy in copies:
        copy.start()
    again1_ref[:tok] = v_ref[...]
    again2_ref[...] = v_ref[...]
    for copy in copies:
        copy.wait()
    pick_rows(groups, k_ref, v_ref, rows_ref, dest_ref, live_ref, kept_ref, again1_ref.at[tok:], onehot)


def by_wraps(body):
    shard = lax.axis_index("ctx")
    for wraps in range(3):
        pl.when((shard == 2 - wraps) if wraps else (shard >= 2))(functools.partial(body, wraps))


def spans_of(wraps, half):
    if wraps == 0:
        return [(0, 2 * half, 4 * half)]
    return [(0, half, (3 - wraps) * half), (half, 2 * half, (4 + wraps) * half)]


def score_kernel(groups, qpk, half, q_ref, k_ref, k2_ref, k1_ref,
                 w_ref, inv_ref, own_ref, back1_ref, back2_ref, xkt, bias, s_buf, col):
    tok = 2 * half
    steps = qpk // STEP_HEADS
    edge = tiles(half)
    late_lo = 3 * half // LANES * LANES
    late_at = 3 * half - late_lo
    col[...] = jnp.zeros_like(col)
    row = lax.broadcasted_iota(jnp.int32, (half, edge), 0)
    column = lax.broadcasted_iota(jnp.int32, (half, edge), 1)
    masks = ((column >= half) | (column <= row), column <= row, column - late_at <= row)
    for i, mask in enumerate(masks):
        bias[i] = jnp.where(mask, 0.0, -jnp.inf)
    cut = jnp.where(lax.broadcasted_iota(jnp.int32, (CHUNK, LANES), 1) < half % LANES, 0.0, -jnp.inf)
    for group in range(groups):
        at = slice(group * HD, (group + 1) * HD)
        xkt[group] = jnp.concatenate(
            [k_ref[:half, at], k1_ref[:half, at], k2_ref[:half, at],
             k_ref[half:, at], k2_ref[half:, at], k1_ref[half:, at]], 0
        ).T

    def attend(wraps, group, step):
        spans = spans_of(wraps, half)

        def scores(i):
            at = pl.ds(pl.multiple_of(((group * steps + step) * STEP_HEADS + i) * HD, HD), HD)
            for first, last, keys in spans:
                s_buf[i, first:last, : tiles(keys)] = jnp.dot(
                    q_ref[first:last, at], xkt[group, :, : tiles(keys)],
                    preferred_element_type=jnp.float32,
                )

        def weights(i):
            head = (group * steps + step) * STEP_HEADS + i
            totals = {}
            for first, last, keys in spans:
                for r in range(first, last, CHUNK):
                    rows = slice(r, r + CHUNK)
                    early = r < half
                    inside = slice(r, r + CHUNK) if early else slice(r - half, r - half + CHUNK)
                    if early:
                        valid = (3 - wraps) * half
                    elif wraps == 0 and inside.stop + 3 * half <= late_lo + LANES:
                        valid = late_lo + LANES
                    else:
                        valid = (4 + wraps) * half
                    parts = []
                    for at in range(0, valid, LANES):
                        part = s_buf[i, rows, at : at + LANES]
                        if early and at < edge:
                            part += bias[1 if wraps == 2 else 0, inside, at : at + LANES]
                        elif not early and late_lo <= at < late_lo + edge:
                            part += bias[2, inside, at - late_lo : at - late_lo + LANES]
                        elif at + LANES > valid:
                            part += cut
                        parts.append(part)
                    peak = wide(jnp.max(functools.reduce(jnp.maximum, parts), axis=1, keepdims=True))
                    parts = [jnp.exp2((part - peak) * EXP2_SCALE) for part in parts]
                    inverse = 1.0 / wide(
                        jnp.sum(functools.reduce(jnp.add, parts), axis=1, keepdims=True)
                    )
                    inv_ref[head, rows] = inverse
                    for j, part in enumerate(parts):
                        w_ref[head, rows, j * LANES : (j + 1) * LANES] = part.astype(jnp.bfloat16)
                        part = folded(part * inverse)
                        totals[j] = totals[j] + part if j in totals else part
                    if len(parts) * LANES < tiles(keys):
                        w_ref[head, rows, len(parts) * LANES : tiles(keys)] = jnp.zeros(
                            (CHUNK, tiles(keys) - len(parts) * LANES), jnp.bfloat16
                        )
            for j, block in totals.items():
                col[:, j * LANES : (j + 1) * LANES] += block

        scores(0)
        for i in range(STEP_HEADS):
            if i + 1 < STEP_HEADS:
                scores(i + 1)
            weights(i)

    @by_wraps
    def _(wraps):
        for group in range(groups):
            pl.loop(0, steps)(functools.partial(attend, wraps, group))

    total = jnp.sum(col[...], axis=0, keepdims=True) * (1.0 / QH)
    own_ref[:, :half] = total[:, :half]
    own_ref[:, half:] = total[:, 3 * half : 4 * half]
    back1_ref[:, :half] = total[:, half : 2 * half]
    back1_ref[:, half:] = total[:, 5 * half :]
    back2_ref[:, :half] = total[:, 2 * half : 3 * half]
    back2_ref[:, half:] = total[:, 4 * half : 5 * half]


def value_kernel(group, qpk, half, v_ref, v1_ref, v2_ref, w_ref, inv_ref, pass_ref, *refs):
    tok = 2 * half
    steps = qpk // STEP_HEADS
    out_hbm, again_ref, xv, out_buf, sems = refs[-5:]
    again_ref[...] = pass_ref[...]
    at = slice(group * HD, (group + 1) * HD)
    xv[...] = jnp.concatenate(
        [v_ref[:half, at], v1_ref[:half, at], v2_ref[:half, at],
         v_ref[half:, at], v2_ref[half:, at], v1_ref[half:tok, at]], 0
    )

    def sent(step):
        first = (group * steps + step) * STEP_HEADS * HD
        at = pl.ds(pl.multiple_of(first, HD), STEP_HEADS * HD)
        return pltpu.make_async_copy(out_buf.at[step], out_hbm.at[:, at], sems.at[step])

    def attend(wraps, step):
        for i in range(STEP_HEADS):
            lanes = slice(i * HD, (i + 1) * HD)
            head = (group * steps + step) * STEP_HEADS + i
            for first, last, keys in spans_of(wraps, half):
                product = jnp.dot(
                    w_ref[head, first:last, : tiles(keys)], xv[: tiles(keys)],
                    preferred_element_type=jnp.float32,
                )
                out_buf[step, first:last, lanes] = (product * inv_ref[head, first:last]).astype(
                    jnp.bfloat16
                )
        sent(step).start()

    @by_wraps
    def _(wraps):
        pl.loop(0, steps)(functools.partial(attend, wraps))

    @pl.loop(0, steps)
    def _(step):
        sent(step).wait()


def cost(pairs, heads, half):
    return pl.CostEstimate(
        flops=heads * pairs * half * half * HD * 12,
        bytes_accessed=heads * half * HD * 64,
        transcendentals=heads * pairs * half * half,
    )


def keep(keys, values, *kept):
    tok = keys.shape[0]
    groups = keys.shape[1] // HD
    count = kept[1].shape[2]
    rows = groups * count // 2 * KB
    shapes = [
        jax.ShapeDtypeStruct((rows, 2 * HD), values.dtype),
        jax.ShapeDtypeStruct((tok + rows, groups * HD), values.dtype),
        jax.ShapeDtypeStruct(values.shape, values.dtype),
    ]
    shapes += [jax.ShapeDtypeStruct((groups * KB, 2 * HD), jnp.int32)] * (count.bit_length() - 1)
    return pl.pallas_call(
        functools.partial(keep_kernel, groups),
        out_shape=shapes,
        in_specs=[VMEM] * 2 + [HBM] * 3,
        out_specs=[VMEM] * len(shapes),
        scratch_shapes=[pltpu.SMEM(a.shape, a.dtype) for a in kept]
        + [pltpu.VMEM((groups, 2 * rows, tok), jnp.float32), pltpu.SemaphoreType.DMA((3,))],
        compiler_params=pltpu.CompilerParams(vmem_limit_bytes=8 * MIB),
        cost_estimate=cost(2, 16, tok // 2),
        name="keep_rows",
    )(keys, values, *kept)


def window_scores(queries, keys, k2, k1):
    tok, width = queries.shape
    half = tok // 2
    groups = keys.shape[1] // HD
    heads = width // HD
    most = 6 * half
    return pl.pallas_call(
        functools.partial(score_kernel, groups, heads // groups, half),
        out_shape=(
            jax.ShapeDtypeStruct((heads, tok, most), jnp.bfloat16),
            jax.ShapeDtypeStruct((heads, tok, LANES), jnp.float32),
            jax.ShapeDtypeStruct((1, tok), jnp.float32),
            jax.ShapeDtypeStruct((1, tok), jnp.float32),
            jax.ShapeDtypeStruct((1, tok), jnp.float32),
        ),
        in_specs=[VMEM] * 4,
        out_specs=(VMEM,) * 5,
        scratch_shapes=[
            pltpu.VMEM((groups, HD, most), jnp.bfloat16),
            pltpu.VMEM((3, half, tiles(half)), jnp.float32),
            pltpu.VMEM((STEP_HEADS, tok, most), jnp.float32),
            pltpu.VMEM((8, most), jnp.float32),
        ],
        compiler_params=pltpu.CompilerParams(vmem_limit_bytes=20 * MIB),
        cost_estimate=cost(7, heads, half),
        name="window_scores",
    )(queries, keys, k2, k1)


def ride(back, kept, v1):
    tok = back.shape[1]
    rows, width = kept.shape
    size = rows // 2
    top = groups_of_eight(pl.cdiv(tok, width))

    def kernel(back_ref, kept_ref, v1_ref, out_ref, stay_ref):
        out_ref[:top] = jnp.zeros((top, width), jnp.float32)
        for i in range(pl.cdiv(tok, width)):
            part = back_ref[:, i * width : min((i + 1) * width, tok)]
            out_ref[i : i + 1, : part.shape[1]] = part
        mine = (lax.axis_index("ctx") >> 1) % 2 == 1
        for i, (low, high) in enumerate(
            ((kept_ref[:size], kept_ref[size:]), (v1_ref[tok : tok + size], v1_ref[tok + size :]))
        ):
            stay_ref[i * size : (i + 1) * size] = jnp.where(mine, high, low)
            out_ref[top + i * size : top + (i + 1) * size] = jnp.where(mine, low, high).astype(jnp.float32)

    return pl.pallas_call(
        kernel,
        out_shape=(
            jax.ShapeDtypeStruct((top + rows, width), jnp.float32),
            jax.ShapeDtypeStruct((rows, width), kept.dtype),
        ),
        in_specs=[VMEM] * 3,
        out_specs=(VMEM,) * 2,
        compiler_params=pltpu.CompilerParams(vmem_limit_bytes=4 * MIB),
        name="ride",
    )(back, kept, v1)


def groups_of_eight(rows):
    return (rows + 7) // 8 * 8


def window_values(group, values, v1, v2, weights, inverse, passed, *attended):
    heads, tok, most = weights.shape
    groups = values.shape[1] // HD
    steps = heads // groups // STEP_HEADS
    return pl.pallas_call(
        functools.partial(value_kernel, group, heads // groups, tok // 2),
        out_shape=(
            jax.ShapeDtypeStruct((tok, heads * HD), jnp.bfloat16),
            jax.ShapeDtypeStruct(passed.shape, passed.dtype),
        ),
        in_specs=[VMEM] * 6 + [HBM] * len(attended),
        out_specs=(HBM, VMEM),
        scratch_shapes=[
            pltpu.VMEM((most, HD), jnp.bfloat16),
            pltpu.VMEM((steps, tok, STEP_HEADS * HD), jnp.bfloat16),
            pltpu.SemaphoreType.DMA((steps,)),
        ],
        input_output_aliases={6: 0} if attended else {},
        compiler_params=pltpu.CompilerParams(vmem_limit_bytes=12 * MIB),
        cost_estimate=cost(3, heads // groups, tok // 2),
        name="window_values",
    )(values, v1, v2, weights, inverse, passed, *attended)


def on_device(queries, keys, values, keep_rows, keep_dest, keep_count):
    count = lax.axis_size("ctx")
    heads = lax.axis_size("head")
    groups = keys.shape[1] // HD

    def along(block, distance):
        return lax.ppermute(block, "ctx", [(i, (i + distance) % count) for i in range(count)])

    def swap(block, axis, bit):
        return lax.ppermute(block, axis, [(i, i ^ bit) for i in range(lax.axis_size(axis))])

    k2 = along(keys, 2)
    k1 = along(keys, 1)
    kept, again1, again2, *bits = keep(
        keys, values, jnp.swapaxes(keep_rows, 2, 3), keep_dest, keep_count
    )
    v1 = along(again1, 1)
    v2 = along(again2, 2)
    weights, inverse, own, back1, back2 = window_scores(queries, keys, k2, k1)
    tok = keys.shape[0]
    riding, stay = ride(back2, kept, v1)
    back1, riding = along(back1, -1), along(riding, -2)
    attended, own = window_values(0, values, v1, v2, weights, inverse, own)
    width = riding.shape[1]
    top = riding.shape[0] - stay.shape[0]
    back2 = jnp.concatenate([riding[i : i + 1] for i in range(pl.cdiv(tok, width))], 1)[:, :tok]
    scores = own + back1 + back2

    shape = (1, 1, 2, -1, groups * KB, width)
    blocks = jnp.concatenate(
        [stay.reshape(shape), riding[top:].astype(stay.dtype).reshape(shape)], axis=1
    )
    flags = [bit > 0 for bit in bits]
    bit = 1
    while 2 << bit <= count or 1 << bit <= heads:
        if 4 << bit <= count:
            low, high = jnp.split(blocks, 2, axis=3)
            mine = flags[bit + 1]
            stay, sent = jnp.where(mine, high, low), jnp.where(mine, low, high)
            found = swap(sent, "ctx", 2 << bit)
            blocks = jnp.concatenate([jnp.where(mine, found, stay), jnp.where(mine, stay, found)])
        if 1 << bit <= heads:
            other = swap(scores, "head", 1 << bit - 1)
            if 2 << bit > heads:
                for group in range(1, groups):
                    attended, scores = window_values(
                        group, values, v1, v2, weights, inverse, scores, attended
                    )
            scores = scores + other
        bit += 1

    def merged(even, odd):
        return jnp.stack([even, odd], axis=1).reshape((-1,) + even.shape[1:])

    blocks = blocks[:, :, :, 0]
    same, above = blocks[:, 0], blocks[:, 1]
    blocks = merged(
        jnp.where(flags[1], jnp.roll(above, 1, axis=0), same), jnp.where(flags[1], same, above)
    )
    near, carried = blocks[:, 0], blocks[:, 1]
    decode_cache = merged(
        jnp.where(flags[0], carried, near), jnp.where(flags[0], near, jnp.roll(carried, -1, axis=0))
    )
    decode_cache = decode_cache.reshape(1, count, KB, groups, width)
    return (attended, scores.reshape(-1), decode_cache)


def solution(mesh):
    return jax.shard_map(
        on_device,
        mesh=mesh,
        in_specs=(
            P("ctx", "head"),
            P("ctx", "head"),
            P("ctx", "head"),
            P("ctx", "head", None, None),
            P("ctx", "head", None),
            P("ctx", "head", None),
        ),
        out_specs=(P("ctx", "head"), P("ctx"), P("ctx", None, None, "head", None)),
        check_vma=False,
    )
```

```python
import functools
import math

import jax
import jax.numpy as jnp
from jax import lax
from jax.experimental import pallas as pl
from jax.experimental.pallas import tpu as pltpu
from jax.sharding import PartitionSpec as P

HD = 128
KB = 4
QH = 64
LANES = 128
CHUNK = 32
STEP_HEADS = 4
EXP2_SCALE = HD ** (-0.5) * math.log2(math.e)
VMEM = pl.BlockSpec(memory_space=pltpu.VMEM)
HBM = pl.BlockSpec(memory_space=pltpu.HBM)
MIB = 1024 * 1024


def tiles(width):
    return pl.cdiv(width, LANES) * LANES


def wide(column):
    return jnp.broadcast_to(column, (CHUNK, LANES))


def folded(block):
    return jnp.sum(block.reshape(-1, 8, LANES), axis=0)


def pick_rows(groups, k_ref, v_ref, rows_ref, dest_ref, live_ref, kept_ref, sent_ref, onehot):
    tok = k_ref.shape[0]
    me = lax.axis_index("ctx")
    count = dest_ref.shape[2]
    bits = count.bit_length() - 2
    size = kept_ref.shape[0]
    lanes = lax.broadcasted_iota(jnp.int32, (1, tok), 1)
    onehot[...] = jnp.zeros_like(onehot)
    for group in range(groups):
        @pl.loop(0, count, unroll=4)
        def _(j):
            dest = dest_ref[0, group, j]
            place = (dest + me) % 2
            for bit in range(bits):
                place = 2 * place + (dest >> (bit + 1)) % 2
            for slot in range(KB):
                row = jnp.where(slot < live_ref[0, group, j], rows_ref[0, group, slot, j], -1)
                at = (place * KB + slot) * groups + group
                onehot[group, pl.ds(at, 1)] = (lanes == row).astype(jnp.float32)
    for first, picked_ref in ((0, kept_ref), (size, sent_ref)):
        for ref, lane in ((k_ref, 0), (v_ref, HD)):
            picked_ref[:, lane : lane + HD] = sum(
                jnp.dot(
                    onehot[group, first : first + size].astype(jnp.bfloat16),
                    ref[:, group * HD : (group + 1) * HD],
                    preferred_element_type=jnp.float32,
                )
                for group in range(groups)
            ).astype(jnp.bfloat16)


def keep_kernel(groups, k_ref, v_ref, rows_hbm, dest_hbm, live_hbm, kept_ref, again1_ref, again2_ref, *refs):
    tok = k_ref.shape[0]
    *bit_refs, rows_ref, dest_ref, live_ref, onehot, sems = refs
    me = lax.axis_index("ctx")
    for bit, bit_ref in enumerate(bit_refs):
        bit_ref[...] = jnp.broadcast_to((me >> bit) % 2, bit_ref.shape)
    copies = [
        pltpu.make_async_copy(src, dst, sems.at[i])
        for i, (src, dst) in enumerate(
            ((rows_hbm, rows_ref), (dest_hbm, dest_ref), (live_hbm, live_ref))
        )
    ]
    for copy in copies:
        copy.start()
    again1_ref[:tok] = v_ref[...]
    again2_ref[...] = v_ref[...]
    for copy in copies:
        copy.wait()
    pick_rows(groups, k_ref, v_ref, rows_ref, dest_ref, live_ref, kept_ref, again1_ref.at[tok:], onehot)


def by_wraps(body):
    shard = lax.axis_index("ctx")
    for wraps in range(3):
        pl.when((shard == 2 - wraps) if wraps else (shard >= 2))(functools.partial(body, wraps))


def spans_of(wraps, half):
    if wraps == 0:
        return [(0, 2 * half, 4 * half)]
    return [(0, half, (4 - wraps) * half if wraps == 1 else 2 * half), (half, 2 * half, (4 + wraps) * half)]


def remote_of(wraps, half):
    return (
        [(0, 2 * half, 2 * half)],
        [(0, half, half), (half, 2 * half, 3 * half)],
        [(half, 2 * half, 4 * half)],
    )[wraps]


def local_kernel(groups, qpk, half, q_ref, k_ref, w_ref, top_ref, sum_ref, xkt, bias, s_buf):
    tok = 2 * half
    steps = qpk // STEP_HEADS
    row = lax.broadcasted_iota(jnp.int32, (tok, tok), 0)
    column = lax.broadcasted_iota(jnp.int32, (tok, tok), 1)
    bias[...] = jnp.where(column <= row, 0.0, -jnp.inf)
    for group in range(groups):
        xkt[group] = k_ref[:, group * HD : (group + 1) * HD].T

    @pl.loop(0, groups * steps)
    def _(step):
        group = step // steps

        def scores(i):
            at = pl.ds(pl.multiple_of((step * STEP_HEADS + i) * HD, HD), HD)
            s_buf[i] = jnp.dot(q_ref[:, at], xkt[group], preferred_element_type=jnp.float32)

        def weights(i):
            head = step * STEP_HEADS + i
            for r in range(0, tok, CHUNK):
                rows = slice(r, r + CHUNK)
                parts = []
                for at in range(0, tiles(r + CHUNK), LANES):
                    part = s_buf[i, rows, at : at + LANES]
                    parts.append(part + bias[rows, at : at + LANES] if at + LANES > r else part)
                top = wide(jnp.max(functools.reduce(jnp.maximum, parts), axis=1, keepdims=True))
                parts = [jnp.exp2((part - top) * EXP2_SCALE) for part in parts]
                top_ref[head, rows] = top
                sum_ref[head, rows] = wide(
                    jnp.sum(functools.reduce(jnp.add, parts), axis=1, keepdims=True)
                )
                for j, part in enumerate(parts):
                    w_ref[head, rows, j * LANES : (j + 1) * LANES] = part.astype(jnp.bfloat16)

        scores(0)
        for i in range(STEP_HEADS):
            if i + 1 < STEP_HEADS:
                scores(i + 1)
            weights(i)


def score_kernel(groups, qpk, half, q_ref, k2_ref, k1_ref, wl_ref, top_ref, sum_ref,
                 w_ref, inv_ref, own_ref, back1_ref, back2_ref, xkt, s_buf, col):
    tok = 2 * half
    steps = qpk // STEP_HEADS
    col[...] = jnp.zeros_like(col)
    cut = jnp.where(lax.broadcasted_iota(jnp.int32, (CHUNK, LANES), 1) < half % LANES, 0.0, -jnp.inf)
    for group in range(groups):
        at = slice(group * HD, (group + 1) * HD)
        xkt[group] = jnp.concatenate(
            [k1_ref[:half, at], k2_ref[:half, at], k2_ref[half:, at], k1_ref[half:, at]], 0
        ).T

    def attend(wraps, group, step):
        spans = remote_of(wraps, half)

        def scores(i):
            at = pl.ds(pl.multiple_of(((group * steps + step) * STEP_HEADS + i) * HD, HD), HD)
            for first, last, keys in spans:
                s_buf[i, first:last, : tiles(keys)] = jnp.dot(
                    q_ref[first:last, at], xkt[group, :, : tiles(keys)],
                    preferred_element_type=jnp.float32,
                )

        def weights(i):
            head = (group * steps + step) * STEP_HEADS + i
            totals = {}

            def add(j, part):
                part = folded(part)
                totals[j] = totals[j] + part if j in totals else part

            def merge_local(rows, scale, inverse):
                inv_ref[head, rows] = inverse
                live = tiles(rows.stop)
                for at in range(0, live, LANES):
                    part = wl_ref[head, rows, at : at + LANES]
                    if scale is None:
                        w_ref[head, rows, at : at + LANES] = part
                        part = part.astype(jnp.float32)
                    else:
                        part = part.astype(jnp.float32) * scale
                        w_ref[head, rows, at : at + LANES] = part.astype(jnp.bfloat16)
                    add(at // LANES, part * inverse)
                if live < tok:
                    w_ref[head, rows, live:tok] = jnp.zeros((CHUNK, tok - live), jnp.bfloat16)

            if wraps == 2:
                for r in range(0, half, CHUNK):
                    rows = slice(r, r + CHUNK)
                    merge_local(rows, None, 1.0 / sum_ref[head, rows])
            for first, last, keys in spans:
                for r in range(first, last, CHUNK):
                    rows = slice(r, r + CHUNK)
                    parts = []
                    for at in range(0, keys, LANES):
                        part = s_buf[i, rows, at : at + LANES]
                        parts.append(part + cut if at + LANES > keys else part)
                    top = wide(jnp.max(functools.reduce(jnp.maximum, parts), axis=1, keepdims=True))
                    top_l = top_ref[head, rows]
                    top = jnp.maximum(top, top_l)
                    scale = jnp.exp2((top_l - top) * EXP2_SCALE)
                    parts = [jnp.exp2((part - top) * EXP2_SCALE) for part in parts]
                    total = wide(jnp.sum(functools.reduce(jnp.add, parts), axis=1, keepdims=True))
                    inverse = 1.0 / (sum_ref[head, rows] * scale + total)
                    for j, part in enumerate(parts):
                        w_ref[head, rows, tok + j * LANES : tok + (j + 1) * LANES] = part.astype(
                            jnp.bfloat16
                        )
                        add(tok // LANES + j, part * inverse)
                    merge_local(rows, scale, inverse)
            for j, block in totals.items():
                col[:, j * LANES : (j + 1) * LANES] += block

        scores(0)
        for i in range(STEP_HEADS):
            if i + 1 < STEP_HEADS:
                scores(i + 1)
            weights(i)

    @by_wraps
    def _(wraps):
        for group in range(groups):
            pl.loop(0, steps)(functools.partial(attend, wraps, group))

    total = jnp.sum(col[...], axis=0, keepdims=True) * (1.0 / QH)
    own_ref[...] = total[:, :tok]
    back1_ref[:, :half] = total[:, tok : tok + half]
    back1_ref[:, half:] = total[:, tok + 3 * half :]
    back2_ref[...] = total[:, tok + half : tok + 3 * half]


def value_kernel(group, qpk, half, v_ref, v1_ref, v2_ref, w_ref, inv_ref, pass_ref, *refs):
    tok = 2 * half
    steps = qpk // STEP_HEADS
    out_hbm, again_ref, xv, out_buf, sems = refs[-5:]
    again_ref[...] = pass_ref[...]
    at = slice(group * HD, (group + 1) * HD)
    xv[...] = jnp.concatenate(
        [v_ref[:, at], v1_ref[:half, at], v2_ref[:half, at], v2_ref[half:, at], v1_ref[half:tok, at]], 0
    )

    def sent(step):
        first = (group * steps + step) * STEP_HEADS * HD
        at = pl.ds(pl.multiple_of(first, HD), STEP_HEADS * HD)
        return pltpu.make_async_copy(out_buf.at[step], out_hbm.at[:, at], sems.at[step])

    def attend(wraps, step):
        for i in range(STEP_HEADS):
            lanes = slice(i * HD, (i + 1) * HD)
            head = (group * steps + step) * STEP_HEADS + i
            for first, last, keys in spans_of(wraps, half):
                product = jnp.dot(
                    w_ref[head, first:last, : tiles(keys)], xv[: tiles(keys)],
                    preferred_element_type=jnp.float32,
                )
                out_buf[step, first:last, lanes] = (product * inv_ref[head, first:last]).astype(
                    jnp.bfloat16
                )
        sent(step).start()

    @by_wraps
    def _(wraps):
        pl.loop(0, steps)(functools.partial(attend, wraps))

    @pl.loop(0, steps)
    def _(step):
        sent(step).wait()


def cost(pairs, heads, half):
    return pl.CostEstimate(
        flops=heads * pairs * half * half * HD * 12,
        bytes_accessed=heads * half * HD * 64,
        transcendentals=heads * pairs * half * half,
    )


def keep(keys, values, *kept):
    tok = keys.shape[0]
    groups = keys.shape[1] // HD
    count = kept[1].shape[2]
    rows = groups * count // 2 * KB
    shapes = [
        jax.ShapeDtypeStruct((rows, 2 * HD), values.dtype),
        jax.ShapeDtypeStruct((tok + rows, groups * HD), values.dtype),
        jax.ShapeDtypeStruct(values.shape, values.dtype),
    ]
    shapes += [jax.ShapeDtypeStruct((groups * KB, 2 * HD), jnp.int32)] * (count.bit_length() - 1)
    return pl.pallas_call(
        functools.partial(keep_kernel, groups),
        out_shape=shapes,
        in_specs=[VMEM] * 2 + [HBM] * 3,
        out_specs=[VMEM] * len(shapes),
        scratch_shapes=[pltpu.SMEM(a.shape, a.dtype) for a in kept]
        + [pltpu.VMEM((groups, 2 * rows, tok), jnp.float32), pltpu.SemaphoreType.DMA((3,))],
        compiler_params=pltpu.CompilerParams(vmem_limit_bytes=8 * MIB),
        cost_estimate=cost(2, 16, tok // 2),
        name="keep_rows",
    )(keys, values, *kept)


def local_scores(queries, keys):
    tok, width = queries.shape
    groups = keys.shape[1] // HD
    heads = width // HD
    spread = jax.ShapeDtypeStruct((heads, tok, LANES), jnp.float32)
    return pl.pallas_call(
        functools.partial(local_kernel, groups, heads // groups, tok // 2),
        out_shape=(jax.ShapeDtypeStruct((heads, tok, tok), jnp.bfloat16), spread, spread),
        in_specs=[VMEM] * 2,
        out_specs=(VMEM,) * 3,
        scratch_shapes=[
            pltpu.VMEM((groups, HD, tok), jnp.bfloat16),
            pltpu.VMEM((tok, tok), jnp.float32),
            pltpu.VMEM((STEP_HEADS, tok, tok), jnp.float32),
        ],
        compiler_params=pltpu.CompilerParams(vmem_limit_bytes=12 * MIB),
        cost_estimate=cost(3, heads, tok // 2),
        name="local_scores",
    )(queries, keys)


def remote_scores(queries, k2, k1, *local):
    tok, width = queries.shape
    half = tok // 2
    groups = k1.shape[1] // HD
    heads = width // HD
    line = jax.ShapeDtypeStruct((1, tok), jnp.float32)
    return pl.pallas_call(
        functools.partial(score_kernel, groups, heads // groups, half),
        out_shape=(
            jax.ShapeDtypeStruct((heads, tok, 6 * half), jnp.bfloat16),
            jax.ShapeDtypeStruct((heads, tok, LANES), jnp.float32),
            line,
            line,
            line,
        ),
        in_specs=[VMEM] * 6,
        out_specs=(VMEM,) * 5,
        scratch_shapes=[
            pltpu.VMEM((groups, HD, 4 * half), jnp.bfloat16),
            pltpu.VMEM((STEP_HEADS, tok, 4 * half), jnp.float32),
            pltpu.VMEM((8, 6 * half), jnp.float32),
        ],
        compiler_params=pltpu.CompilerParams(vmem_limit_bytes=16 * MIB),
        cost_estimate=cost(4, heads, half),
        name="remote_scores",
    )(queries, k2, k1, *local)


def ride(back, kept, v1):
    tok = back.shape[1]
    rows, width = kept.shape
    size = rows // 2
    top = groups_of_eight(pl.cdiv(tok, width))

    def kernel(back_ref, kept_ref, v1_ref, out_ref, stay_ref):
        out_ref[:top] = jnp.zeros((top, width), jnp.float32)
        for i in range(pl.cdiv(tok, width)):
            part = back_ref[:, i * width : min((i + 1) * width, tok)]
            out_ref[i : i + 1, : part.shape[1]] = part
        mine = (lax.axis_index("ctx") >> 1) % 2 == 1
        for i, (low, high) in enumerate(
            ((kept_ref[:size], kept_ref[size:]), (v1_ref[tok : tok + size], v1_ref[tok + size :]))
        ):
            stay_ref[i * size : (i + 1) * size] = jnp.where(mine, high, low)
            out_ref[top + i * size : top + (i + 1) * size] = jnp.where(mine, low, high).astype(jnp.float32)

    return pl.pallas_call(
        kernel,
        out_shape=(
            jax.ShapeDtypeStruct((top + rows, width), jnp.float32),
            jax.ShapeDtypeStruct((rows, width), kept.dtype),
        ),
        in_specs=[VMEM] * 3,
        out_specs=(VMEM,) * 2,
        compiler_params=pltpu.CompilerParams(vmem_limit_bytes=4 * MIB),
        name="ride",
    )(back, kept, v1)


def groups_of_eight(rows):
    return (rows + 7) // 8 * 8


def window_values(group, values, v1, v2, weights, inverse, passed, *attended):
    heads, tok, most = weights.shape
    groups = values.shape[1] // HD
    steps = heads // groups // STEP_HEADS
    return pl.pallas_call(
        functools.partial(value_kernel, group, heads // groups, tok // 2),
        out_shape=(
            jax.ShapeDtypeStruct((tok, heads * HD), jnp.bfloat16),
            jax.ShapeDtypeStruct(passed.shape, passed.dtype),
        ),
        in_specs=[VMEM] * 6 + [HBM] * len(attended),
        out_specs=(HBM, VMEM),
        scratch_shapes=[
            pltpu.VMEM((most, HD), jnp.bfloat16),
            pltpu.VMEM((steps, tok, STEP_HEADS * HD), jnp.bfloat16),
            pltpu.SemaphoreType.DMA((steps,)),
        ],
        input_output_aliases={6: 0} if attended else {},
        compiler_params=pltpu.CompilerParams(vmem_limit_bytes=12 * MIB),
        cost_estimate=cost(3, heads // groups, tok // 2),
        name="window_values",
    )(values, v1, v2, weights, inverse, passed, *attended)


def on_device(queries, keys, values, keep_rows, keep_dest, keep_count):
    count = lax.axis_size("ctx")
    heads = lax.axis_size("head")
    groups = keys.shape[1] // HD

    def along(block, distance):
        return lax.ppermute(block, "ctx", [(i, (i + distance) % count) for i in range(count)])

    def swap(block, axis, bit):
        return lax.ppermute(block, axis, [(i, i ^ bit) for i in range(lax.axis_size(axis))])

    k2 = along(keys, 2)
    k1 = along(keys, 1)
    kept, again1, again2, *bits = keep(
        keys, values, jnp.swapaxes(keep_rows, 2, 3), keep_dest, keep_count
    )
    v1 = along(again1, 1)
    v2 = along(again2, 2)
    weights, inverse, own, back1, back2 = remote_scores(
        queries, k2, k1, *local_scores(queries, keys)
    )
    tok = keys.shape[0]
    riding, stay = ride(back2, kept, v1)
    back1, riding = along(back1, -1), along(riding, -2)
    attended, own = window_values(0, values, v1, v2, weights, inverse, own)
    width = riding.shape[1]
    top = riding.shape[0] - stay.shape[0]
    back2 = jnp.concatenate([riding[i : i + 1] for i in range(pl.cdiv(tok, width))], 1)[:, :tok]
    scores = own + back1 + back2

    shape = (1, 1, 2, -1, groups * KB, width)
    blocks = jnp.concatenate(
        [stay.reshape(shape), riding[top:].astype(stay.dtype).reshape(shape)], axis=1
    )
    flags = [bit > 0 for bit in bits]
    bit = 1
    while 2 << bit <= count or 1 << bit <= heads:
        if 4 << bit <= count:
            low, high = jnp.split(blocks, 2, axis=3)
            mine = flags[bit + 1]
            stay, sent = jnp.where(mine, high, low), jnp.where(mine, low, high)
            found = swap(sent, "ctx", 2 << bit)
            blocks = jnp.concatenate([jnp.where(mine, found, stay), jnp.where(mine, stay, found)])
        if 1 << bit <= heads:
            other = swap(scores, "head", 1 << bit - 1)
            if 2 << bit > heads:
                for group in range(1, groups):
                    attended, scores = window_values(
                        group, values, v1, v2, weights, inverse, scores, attended
                    )
            scores = scores + other
        bit += 1

    def merged(even, odd):
        return jnp.stack([even, odd], axis=1).reshape((-1,) + even.shape[1:])

    blocks = blocks[:, :, :, 0]
    same, above = blocks[:, 0], blocks[:, 1]
    blocks = merged(
        jnp.where(flags[1], jnp.roll(above, 1, axis=0), same), jnp.where(flags[1], same, above)
    )
    near, carried = blocks[:, 0], blocks[:, 1]
    decode_cache = merged(
        jnp.where(flags[0], carried, near), jnp.where(flags[0], near, jnp.roll(carried, -1, axis=0))
    )
    decode_cache = decode_cache.reshape(1, count, KB, groups, width)
    return (attended, scores.reshape(-1), decode_cache)


def solution(mesh):
    return jax.shard_map(
        on_device,
        mesh=mesh,
        in_specs=(
            P("ctx", "head"),
            P("ctx", "head"),
            P("ctx", "head"),
            P("ctx", "head", None, None),
            P("ctx", "head", None),
            P("ctx", "head", None),
        ),
        out_specs=(P("ctx", "head"), P("ctx"), P("ctx", None, None, "head", None)),
        check_vma=False,
    )
```

```python
import functools
import math

import jax
import jax.numpy as jnp
from jax import lax
from jax.experimental import pallas as pl
from jax.experimental.pallas import tpu as pltpu
from jax.sharding import PartitionSpec as P

HD = 128
KB = 4
QH = 64
LANES = 128
CHUNK = 32
STEP_HEADS = 8
SLOTS = 4
OUT_HEADS = 2
EXP2_SCALE = HD ** (-0.5) * math.log2(math.e)
VMEM = pl.BlockSpec(memory_space=pltpu.VMEM)
HBM = pl.BlockSpec(memory_space=pltpu.HBM)
MIB = 1024 * 1024


def tiles(width):
    return pl.cdiv(width, LANES) * LANES


def wide(column):
    return jnp.broadcast_to(column, (CHUNK, LANES))


def folded(block):
    return jnp.sum(block.reshape(-1, 8, LANES), axis=0)


def pick_rows(groups, k_ref, v_ref, rows_ref, dest_ref, live_ref, kept_ref, sent_ref, onehot):
    tok = k_ref.shape[0]
    me = lax.axis_index("ctx")
    count = dest_ref.shape[2]
    bits = count.bit_length() - 2
    size = kept_ref.shape[0]
    lanes = lax.broadcasted_iota(jnp.int32, (1, tok), 1)
    onehot[...] = jnp.zeros_like(onehot)
    for group in range(groups):
        @pl.loop(0, count, unroll=4)
        def _(j):
            dest = dest_ref[0, group, j]
            place = (dest + me) % 2
            for bit in range(bits):
                place = 2 * place + (dest >> (bit + 1)) % 2
            for slot in range(KB):
                row = jnp.where(slot < live_ref[0, group, j], rows_ref[0, group, slot, j], -1)
                at = (place * KB + slot) * groups + group
                onehot[group, pl.ds(at, 1)] = (lanes == row).astype(jnp.float32)
    for first, picked_ref in ((0, kept_ref), (size, sent_ref)):
        for ref, lane in ((k_ref, 0), (v_ref, HD)):
            picked_ref[:, lane : lane + HD] = sum(
                jnp.dot(
                    onehot[group, first : first + size].astype(jnp.bfloat16),
                    ref[:, group * HD : (group + 1) * HD],
                    preferred_element_type=jnp.float32,
                )
                for group in range(groups)
            ).astype(jnp.bfloat16)


def keep_kernel(groups, k_ref, v_ref, rows_hbm, dest_hbm, live_hbm, kept_ref, again1_ref, again2_ref, *refs):
    tok = k_ref.shape[0]
    *bit_refs, rows_ref, dest_ref, live_ref, onehot, sems = refs
    me = lax.axis_index("ctx")
    for bit, bit_ref in enumerate(bit_refs):
        bit_ref[...] = jnp.broadcast_to((me >> bit) % 2, bit_ref.shape)
    copies = [
        pltpu.make_async_copy(src, dst, sems.at[i])
        for i, (src, dst) in enumerate(
            ((rows_hbm, rows_ref), (dest_hbm, dest_ref), (live_hbm, live_ref))
        )
    ]
    for copy in copies:
        copy.start()
    again1_ref[:tok] = v_ref[...]
    again2_ref[...] = v_ref[...]
    for copy in copies:
        copy.wait()
    pick_rows(groups, k_ref, v_ref, rows_ref, dest_ref, live_ref, kept_ref, again1_ref.at[tok:], onehot)


def by_wraps(body):
    shard = lax.axis_index("ctx")
    for wraps in range(3):
        pl.when((shard == 2 - wraps) if wraps else (shard >= 2))(functools.partial(body, wraps))


def spans_of(wraps, half):
    if wraps == 0:
        return [(0, 2 * half, 4 * half)]
    return [(0, half, (4 - wraps) * half if wraps == 1 else 2 * half), (half, 2 * half, (4 + wraps) * half)]


def local_kernel(groups, qpk, half, q_ref, k_ref, w_ref, top_ref, sum_ref, xkt, bias, s_buf):
    tok = 2 * half
    steps = qpk // STEP_HEADS
    @pl.when(lax.axis_index("ctx") == 0)
    def _():
        row = lax.broadcasted_iota(jnp.int32, (tok, tok), 0)
        column = lax.broadcasted_iota(jnp.int32, (tok, tok), 1)
        bias[...] = jnp.where(column <= row, 0.0, -jnp.inf)
        for group in range(groups):
            xkt[group] = k_ref[:, group * HD : (group + 1) * HD].T

        @pl.loop(0, groups * steps)
        def _(step):
            group = step // steps

            def scores(i):
                at = pl.ds(pl.multiple_of((step * STEP_HEADS + i) * HD, HD), HD)
                s_buf[i % SLOTS] = jnp.dot(q_ref[:, at], xkt[group], preferred_element_type=jnp.float32)

            def weights(i):
                head = step * STEP_HEADS + i
                for r in range(0, tok, CHUNK):
                    rows = slice(r, r + CHUNK)
                    parts = []
                    for at in range(0, tiles(r + CHUNK), LANES):
                        part = s_buf[i % SLOTS, rows, at : at + LANES]
                        parts.append(part + bias[rows, at : at + LANES] if at + LANES > r else part)
                    top = wide(jnp.max(functools.reduce(jnp.maximum, parts), axis=1, keepdims=True))
                    parts = [jnp.exp2((part - top) * EXP2_SCALE) for part in parts]
                    top_ref[head, rows] = top
                    sum_ref[head, rows] = wide(
                        jnp.sum(functools.reduce(jnp.add, parts), axis=1, keepdims=True)
                    )
                    for j, part in enumerate(parts):
                        w_ref[head, rows, j * LANES : (j + 1) * LANES] = part.astype(jnp.bfloat16)

            scores(0)
            for i in range(STEP_HEADS):
                if i + 1 < STEP_HEADS:
                    scores(i + 1)
                weights(i)


def score_kernel(groups, qpk, half, q_ref, k_ref, k2_ref, k1_ref, wl_ref, top_ref, sum_ref,
                 w_ref, inv_ref, own_ref, back1_ref, back2_ref, xkt, bias, s_buf, col):
    tok = 2 * half
    steps = qpk // STEP_HEADS
    col[...] = jnp.zeros_like(col)
    row = lax.broadcasted_iota(jnp.int32, (tok, tok), 0)
    column = lax.broadcasted_iota(jnp.int32, (tok, tok), 1)
    bias[...] = jnp.where(column <= row, 0.0, -jnp.inf)
    cut = jnp.where(lax.broadcasted_iota(jnp.int32, (CHUNK, LANES), 1) < half % LANES, 0.0, -jnp.inf)
    for group in range(groups):
        at = slice(group * HD, (group + 1) * HD)
        xkt[group] = jnp.concatenate(
            [k_ref[:, at], k1_ref[:half, at], k2_ref[:half, at], k2_ref[half:, at], k1_ref[half:, at]], 0
        ).T

    def attend(wraps, group, step):
        merged = wraps == 2
        spans = spans_of(wraps, half)
        origin = tok if merged else 0
        if merged:
            spans = spans[1:]

        def scores(i):
            at = pl.ds(pl.multiple_of(((group * steps + step) * STEP_HEADS + i) * HD, HD), HD)
            for first, last, keys in spans:
                s_buf[i % SLOTS, first:last, origin : tiles(keys)] = jnp.dot(
                    q_ref[first:last, at], xkt[group, :, origin : tiles(keys)],
                    preferred_element_type=jnp.float32,
                )

        def weights(i):
            head = (group * steps + step) * STEP_HEADS + i
            totals = {}

            def add(at, part):
                part = folded(part)
                totals[at] = totals[at] + part if at in totals else part

            def clear(rows):
                live = tiles(rows.stop)
                if live < tok:
                    w_ref[head, rows, live:tok] = jnp.zeros((CHUNK, tok - live), jnp.bfloat16)

            def merge_local(rows, scale, inverse):
                inv_ref[head, rows] = inverse
                for at in range(0, tiles(rows.stop), LANES):
                    part = wl_ref[head, rows, at : at + LANES]
                    if scale is None:
                        w_ref[head, rows, at : at + LANES] = part
                        part = part.astype(jnp.float32)
                    else:
                        part = part.astype(jnp.float32) * scale
                        w_ref[head, rows, at : at + LANES] = part.astype(jnp.bfloat16)
                    add(at, part * inverse)
                clear(rows)

            if merged:
                for r in range(0, half, CHUNK):
                    rows = slice(r, r + CHUNK)
                    merge_local(rows, None, 1.0 / sum_ref[head, rows])
            for first, last, keys in spans:
                for r in range(first, last, CHUNK):
                    rows = slice(r, r + CHUNK)
                    parts = {}
                    if not merged:
                        for at in range(0, tiles(r + CHUNK), LANES):
                            parts[at] = s_buf[i % SLOTS, rows, at : at + LANES]
                            if at + LANES > r:
                                parts[at] += bias[rows, at : at + LANES]
                    for at in range(tok, keys, LANES):
                        parts[at] = s_buf[i % SLOTS, rows, at : at + LANES]
                        if at + LANES > keys:
                            parts[at] += cut
                    peak = functools.reduce(jnp.maximum, parts.values())
                    top = wide(jnp.max(peak, axis=1, keepdims=True))
                    if merged:
                        top_l = top_ref[head, rows]
                        top = jnp.maximum(top, top_l)
                        scale = jnp.exp2((top_l - top) * EXP2_SCALE)
                    parts = {at: jnp.exp2((part - top) * EXP2_SCALE) for at, part in parts.items()}
                    total = functools.reduce(jnp.add, parts.values())
                    total = wide(jnp.sum(total, axis=1, keepdims=True))
                    if merged:
                        total = sum_ref[head, rows] * scale + total
                    inverse = 1.0 / total
                    for at, part in parts.items():
                        w_ref[head, rows, at : at + LANES] = part.astype(jnp.bfloat16)
                        add(at, part * inverse)
                    if merged:
                        merge_local(rows, scale, inverse)
                    else:
                        inv_ref[head, rows] = inverse
                        clear(rows)
            for at, block in totals.items():
                col[:, at : at + LANES] += block

        scores(0)
        for i in range(STEP_HEADS):
            if i + 1 < STEP_HEADS:
                scores(i + 1)
            weights(i)

    @by_wraps
    def _(wraps):
        for group in range(groups):
            pl.loop(0, steps)(functools.partial(attend, wraps, group))

    total = jnp.sum(col[...], axis=0, keepdims=True) * (1.0 / QH)
    own_ref[...] = total[:, :tok]
    back1_ref[:, :half] = total[:, tok : tok + half]
    back1_ref[:, half:] = total[:, tok + 3 * half :]
    back2_ref[...] = total[:, tok + half : tok + 3 * half]


def value_kernel(group, qpk, half, v_ref, v1_ref, v2_ref, w_ref, inv_ref, pass_ref, *refs):
    tok = 2 * half
    out_hbm, again_ref, xv, out_buf, sems = refs[-5:]
    again_ref[...] = pass_ref[...]
    at = slice(group * HD, (group + 1) * HD)
    xv[...] = jnp.concatenate(
        [v_ref[:, at], v1_ref[:half, at], v2_ref[:half, at], v2_ref[half:, at], v1_ref[half:tok, at]], 0
    )

    def sent(part):
        first = (group * qpk + part * OUT_HEADS) * HD
        at = slice(first, first + OUT_HEADS * HD)
        return pltpu.make_async_copy(out_buf.at[part], out_hbm.at[:, at], sems.at[part])

    @by_wraps
    def _(wraps):
        for i in range(qpk):
            part, inside = divmod(i, OUT_HEADS)
            lanes = slice(inside * HD, (inside + 1) * HD)
            head = group * qpk + i
            for first, last, keys in spans_of(wraps, half):
                product = jnp.dot(
                    w_ref[head, first:last, : tiles(keys)], xv[: tiles(keys)],
                    preferred_element_type=jnp.float32,
                )
                out_buf[part, first:last, lanes] = (product * inv_ref[head, first:last]).astype(
                    jnp.bfloat16
                )
            if inside + 1 == OUT_HEADS:
                sent(part).start()

    for part in range(qpk // OUT_HEADS):
        sent(part).wait()


def cost(pairs, heads, half):
    return pl.CostEstimate(
        flops=heads * pairs * half * half * HD * 12,
        bytes_accessed=heads * half * HD * 64,
        transcendentals=heads * pairs * half * half,
    )


def keep(keys, values, *kept):
    tok = keys.shape[0]
    groups = keys.shape[1] // HD
    count = kept[1].shape[2]
    rows = groups * count // 2 * KB
    shapes = [
        jax.ShapeDtypeStruct((rows, 2 * HD), values.dtype),
        jax.ShapeDtypeStruct((tok + rows, groups * HD), values.dtype),
        jax.ShapeDtypeStruct(values.shape, values.dtype),
    ]
    shapes += [jax.ShapeDtypeStruct((groups * KB, 2 * HD), jnp.int32)] * (count.bit_length() - 1)
    return pl.pallas_call(
        functools.partial(keep_kernel, groups),
        out_shape=shapes,
        in_specs=[VMEM] * 2 + [HBM] * 3,
        out_specs=[VMEM] * len(shapes),
        scratch_shapes=[pltpu.SMEM(a.shape, a.dtype) for a in kept]
        + [pltpu.VMEM((groups, 2 * rows, tok), jnp.float32), pltpu.SemaphoreType.DMA((3,))],
        compiler_params=pltpu.CompilerParams(vmem_limit_bytes=8 * MIB),
        cost_estimate=cost(2, 16, tok // 2),
        name="keep_rows",
    )(keys, values, *kept)


def local_scores(queries, keys):
    tok, width = queries.shape
    groups = keys.shape[1] // HD
    heads = width // HD
    spread = jax.ShapeDtypeStruct((heads, tok, LANES), jnp.float32)
    return pl.pallas_call(
        functools.partial(local_kernel, groups, heads // groups, tok // 2),
        out_shape=(jax.ShapeDtypeStruct((heads, tok, tok), jnp.bfloat16), spread, spread),
        in_specs=[VMEM] * 2,
        out_specs=(VMEM,) * 3,
        scratch_shapes=[
            pltpu.VMEM((groups, HD, tok), jnp.bfloat16),
            pltpu.VMEM((tok, tok), jnp.float32),
            pltpu.VMEM((SLOTS, tok, tok), jnp.float32),
        ],
        compiler_params=pltpu.CompilerParams(vmem_limit_bytes=12 * MIB),
        cost_estimate=cost(3, heads, tok // 2),
        name="local_scores",
    )(queries, keys)


def window_scores(queries, keys, k2, k1, *local):
    tok, width = queries.shape
    half = tok // 2
    groups = k1.shape[1] // HD
    heads = width // HD
    line = jax.ShapeDtypeStruct((1, tok), jnp.float32)
    return pl.pallas_call(
        functools.partial(score_kernel, groups, heads // groups, half),
        out_shape=(
            jax.ShapeDtypeStruct((heads, tok, 6 * half), jnp.bfloat16),
            jax.ShapeDtypeStruct((heads, tok, LANES), jnp.float32),
            line,
            line,
            line,
        ),
        in_specs=[VMEM] * 7,
        out_specs=(VMEM,) * 5,
        scratch_shapes=[
            pltpu.VMEM((groups, HD, 6 * half), jnp.bfloat16),
            pltpu.VMEM((tok, tok), jnp.float32),
            pltpu.VMEM((SLOTS, tok, 6 * half), jnp.float32),
            pltpu.VMEM((8, 6 * half), jnp.float32),
        ],
        compiler_params=pltpu.CompilerParams(vmem_limit_bytes=20 * MIB),
        cost_estimate=cost(7, heads, half),
        name="window_scores",
    )(queries, keys, k2, k1, *local)


def ride(back, kept, v1):
    tok = back.shape[1]
    rows, width = kept.shape
    size = rows // 2
    top = groups_of_eight(pl.cdiv(tok, width))

    def kernel(back_ref, kept_ref, v1_ref, out_ref, stay_ref):
        out_ref[:top] = jnp.zeros((top, width), jnp.float32)
        for i in range(pl.cdiv(tok, width)):
            part = back_ref[:, i * width : min((i + 1) * width, tok)]
            out_ref[i : i + 1, : part.shape[1]] = part
        mine = (lax.axis_index("ctx") >> 1) % 2 == 1
        for i, (low, high) in enumerate(
            ((kept_ref[:size], kept_ref[size:]), (v1_ref[tok : tok + size], v1_ref[tok + size :]))
        ):
            stay_ref[i * size : (i + 1) * size] = jnp.where(mine, high, low)
            out_ref[top + i * size : top + (i + 1) * size] = jnp.where(mine, low, high).astype(jnp.float32)

    return pl.pallas_call(
        kernel,
        out_shape=(
            jax.ShapeDtypeStruct((top + rows, width), jnp.float32),
            jax.ShapeDtypeStruct((rows, width), kept.dtype),
        ),
        in_specs=[VMEM] * 3,
        out_specs=(VMEM,) * 2,
        compiler_params=pltpu.CompilerParams(vmem_limit_bytes=4 * MIB),
        name="ride",
    )(back, kept, v1)


def groups_of_eight(rows):
    return (rows + 7) // 8 * 8


def window_values(group, values, v1, v2, weights, inverse, passed, *attended):
    heads, tok, most = weights.shape
    groups = values.shape[1] // HD
    parts = heads // groups // OUT_HEADS
    return pl.pallas_call(
        functools.partial(value_kernel, group, heads // groups, tok // 2),
        out_shape=(
            jax.ShapeDtypeStruct((tok, heads * HD), jnp.bfloat16),
            jax.ShapeDtypeStruct(passed.shape, passed.dtype),
        ),
        in_specs=[VMEM] * 6 + [HBM] * len(attended),
        out_specs=(HBM, VMEM),
        scratch_shapes=[
            pltpu.VMEM((most, HD), jnp.bfloat16),
            pltpu.VMEM((parts, tok, OUT_HEADS * HD), jnp.bfloat16),
            pltpu.SemaphoreType.DMA((parts,)),
        ],
        input_output_aliases={6: 0} if attended else {},
        compiler_params=pltpu.CompilerParams(vmem_limit_bytes=12 * MIB),
        cost_estimate=cost(3, heads // groups, tok // 2),
        name="window_values",
    )(values, v1, v2, weights, inverse, passed, *attended)


def on_device(queries, keys, values, keep_rows, keep_dest, keep_count):
    count = lax.axis_size("ctx")
    heads = lax.axis_size("head")
    groups = keys.shape[1] // HD

    def along(block, distance):
        return lax.ppermute(block, "ctx", [(i, (i + distance) % count) for i in range(count)])

    def swap(block, axis, bit):
        return lax.ppermute(block, axis, [(i, i ^ bit) for i in range(lax.axis_size(axis))])

    k2 = along(keys, 2)
    k1 = along(keys, 1)
    kept, again1, again2, *bits = keep(
        keys, values, jnp.swapaxes(keep_rows, 2, 3), keep_dest, keep_count
    )
    v1 = along(again1, 1)
    v2 = along(again2, 2)
    weights, inverse, own, back1, back2 = window_scores(
        queries, keys, k2, k1, *local_scores(queries, keys)
    )
    tok = keys.shape[0]
    riding, stay = ride(back2, kept, v1)
    back1, riding = along(back1, -1), along(riding, -2)
    attended, own = window_values(0, values, v1, v2, weights, inverse, own)
    width = riding.shape[1]
    top = riding.shape[0] - stay.shape[0]
    back2 = jnp.concatenate([riding[i : i + 1] for i in range(pl.cdiv(tok, width))], 1)[:, :tok]
    scores = own + back1 + back2

    shape = (1, 1, 2, -1, groups * KB, width)
    blocks = jnp.concatenate(
        [stay.reshape(shape), riding[top:].astype(stay.dtype).reshape(shape)], axis=1
    )
    flags = [bit > 0 for bit in bits]
    bit = 1
    while 2 << bit <= count or 1 << bit <= heads:
        if 4 << bit <= count:
            low, high = jnp.split(blocks, 2, axis=3)
            mine = flags[bit + 1]
            stay, sent = jnp.where(mine, high, low), jnp.where(mine, low, high)
            found = swap(sent, "ctx", 2 << bit)
            blocks = jnp.concatenate([jnp.where(mine, found, stay), jnp.where(mine, stay, found)])
        if 1 << bit <= heads:
            other = swap(scores, "head", 1 << bit - 1)
            if 2 << bit > heads:
                for group in range(1, groups):
                    attended, scores = window_values(
                        group, values, v1, v2, weights, inverse, scores, attended
                    )
            scores = scores + other
        bit += 1

    def merged(even, odd):
        return jnp.stack([even, odd], axis=1).reshape((-1,) + even.shape[1:])

    blocks = blocks[:, :, :, 0]
    same, above = blocks[:, 0], blocks[:, 1]
    blocks = merged(
        jnp.where(flags[1], jnp.roll(above, 1, axis=0), same), jnp.where(flags[1], same, above)
    )
    near, carried = blocks[:, 0], blocks[:, 1]
    decode_cache = merged(
        jnp.where(flags[0], carried, near), jnp.where(flags[0], near, jnp.roll(carried, -1, axis=0))
    )
    decode_cache = decode_cache.reshape(1, count, KB, groups, width)
    return (attended, scores.reshape(-1), decode_cache)


def solution(mesh):
    return jax.shard_map(
        on_device,
        mesh=mesh,
        in_specs=(
            P("ctx", "head"),
            P("ctx", "head"),
            P("ctx", "head"),
            P("ctx", "head", None, None),
            P("ctx", "head", None),
            P("ctx", "head", None),
        ),
        out_specs=(P("ctx", "head"), P("ctx"), P("ctx", None, None, "head", None)),
        check_vma=False,
    )
```
